32 devices in a mesh: grp: 4 (over y, x), tp: 8 (over z, core).
Axes of the slice: x: 2, y: 2, z: 4, core: 2. Of those that a mesh axis runs over, the one named last changes fastest.
Arguments:
- tokens: bfloat16 [384, 5120], P('grp'), may hold values from -36 to 36
- trainer_panels: bfloat16 [32, 5120, 128], P('tp', 'grp'), may hold values from -0.078125 to 0.078125
- panel_home: int32 [24], replicated, may hold values from 0 to 31, as said below
- lengths: int32 [4, 4], P('grp'), may hold values from 1 to 48, 96 in all within a row
Outputs:
- context: float32 [384, 1024], P(('grp', 'tp'))
The draws below stay inside these ranges and needn't reach their ends.
Inputs may be any that keep to these rules, and one draw needn't show every extreme that they name: `panel_home`: entries are distinct; entry p is 4 times the tp index of the trainer device that holds panel p, plus the panel's slot on that device. Panels 0 to 7 are query heads, the next 8 key heads, the last 8 value heads. Some trainer device holds 4 panels.
All inputs are finite; a program needn't handle non-finite values.
Results may differ from the reference program's by a relative error of at most 0.012.
Values may be sent and summed in bfloat16 or wider, within the bound.
No kernel may reach another device: no remote copies, remote signals or barrier semaphores. Data moves between devices by JAX's collectives and lax.ppermute only.
A program may use at most 64 MiB of HBM per device.

```python
import math
import jax
import jax.numpy as jnp
import numpy as np
from jax import lax

D = 5120
HEAD_DIM = 128
KV_HEADS = 8
RESP = 4
HEADS = 8
TOKENS = 96
ALL_TOKENS = 384
MOST_LEN = 48
PANELS = 24
SLOTS = 4
SLOTS_ALL = 32
N_GRP = 4


def draw_tokens(key, part):
    normal_base = jnp.clip(jax.random.normal(key, (ALL_TOKENS, D), jnp.float32), -6.0, 6.0)
    return normal_base.astype(jnp.bfloat16)


def draw_panel_home(key, part):
    panel_order = jax.random.permutation(jax.random.fold_in(key, 11), PANELS)
    full_owner = jax.random.randint(jax.random.fold_in(key, 12), (), 0, SLOTS_ALL // SLOTS)
    free_spots = jax.random.permutation(jax.random.fold_in(key, 13), SLOTS_ALL - SLOTS).astype(jnp.int32)
    free_spots = jnp.where(free_spots >= full_owner * SLOTS, free_spots + SLOTS, free_spots)
    panel_rank = jnp.arange(PANELS, dtype=jnp.int32)
    slot_spot = jnp.where(panel_rank < SLOTS, full_owner * SLOTS + panel_rank, free_spots[jnp.maximum(panel_rank - SLOTS, 0)])
    home_slots = jnp.zeros((PANELS,), jnp.int32).at[panel_order].set(slot_spot.astype(jnp.int32))
    return home_slots


def block_levels(stream_key, extent, pieces, least, high):
    loudness, own = 1.0, jax.random.fold_in(stream_key, 6)
    for axis_at, blocks in pieces:
        heights = jnp.exp(jax.random.uniform(jax.random.fold_in(own, axis_at), (blocks,), jnp.float32, least / len(pieces), high / len(pieces)))
        loudness = loudness * jnp.repeat(heights, extent[axis_at] // blocks).reshape([-1 if axis == axis_at else 1 for axis in range(len(extent))])
    return loudness


def split_up(amount, total, bound, lean):
    loads = [(1 << 20) // math.isqrt(standing ** lean) + 1 for standing in range(2, amount + 1)]
    rest, counts = total - bound - (amount - 1), [1] * (amount - 1)
    while rest > 0:
        free = [i for i in range(amount - 1) if counts[i] < bound]
        pool, budget = sum([loads[i] for i in free]), rest
        for i in free:
            more = min(bound - counts[i], max(1, budget * loads[i] // pool), rest)
            counts[i] = counts[i] + more
            rest = rest - more
    return np.array([bound] + counts)


def ragged_sizes(rng, number_of, total, limit, slope):
    if number_of == 2:
        one = jax.random.randint(rng, (), max(1, total - limit), min(limit, total - 1) + 1)
        return jnp.stack([one, total - one])
    sizes = jnp.asarray(split_up(number_of, total, limit, slope), jnp.int32)
    couples = (number_of - 1) // 2
    source_of, sink = sizes[1:1 + 2 * couples:2], sizes[2:2 + 2 * couples:2]
    margin = jnp.minimum(source_of - 1, limit - sink)
    moved = jax.random.randint(jax.random.fold_in(rng, 1), (couples,), 0, 1 << 20) % (margin + 1)
    sizes = sizes.at[1:1 + 2 * couples:2].set(source_of - moved).at[2:2 + 2 * couples:2].set(sink + moved)
    return sizes[jax.random.permutation(jax.random.fold_in(rng, 2), number_of)]


def normal_values(rng, dims, scale, most, shards=(), held_as=jnp.bfloat16):
    level = block_levels(rng, dims, shards, -0.22, 0.18) if shards else 1.0
    values = jax.random.normal(rng, dims, jnp.float32) * scale * level
    return jnp.minimum(jnp.maximum(values, -most), most).astype(held_as)


def setup_inputs(seed: int = 0) -> dict:
    keys = jax.random.split(jax.random.key(seed), 5)
    tokens = draw_tokens(jax.random.fold_in(keys[4], 71), 0)
    trainer_panels = normal_values(keys[1], (SLOTS_ALL, D, HEAD_DIM), D ** -0.5, 0.078125, ((0, 8), (1, 4)))
    panel_home = draw_panel_home(jax.random.fold_in(keys[4], 71), 0)
    lengths = jax.vmap(lambda own: ragged_sizes(own, RESP, TOKENS, MOST_LEN, 2))(jax.random.split(keys[3], N_GRP)).reshape((N_GRP, RESP)).astype(jnp.int32)
    return dict(tokens=tokens, trainer_panels=trainer_panels, panel_home=panel_home, lengths=lengths)


def reference(tokens, trainer_panels, panel_home, lengths):
    group_size = HEADS // KV_HEADS
    stacked = trainer_panels[panel_home]
    weights = jnp.transpose(stacked, (1, 0, 2)).reshape(D, PANELS * HEAD_DIM)
    score_scale = HEAD_DIM ** -0.5
    head_ids = jnp.arange(HEADS, dtype=jnp.int32)
    kv_panel = HEADS + head_ids // group_size
    position = jnp.arange(TOKENS, dtype=jnp.int32)
    outputs = []
    for group_id in range(N_GRP):
        group_rows = tokens[group_id * TOKENS:(group_id + 1) * TOKENS]
        projected = jnp.dot(group_rows, weights, preferred_element_type=jnp.float32).astype(jnp.bfloat16)
        projected = lax.optimization_barrier(projected)
        projected = projected.astype(jnp.float32).reshape(TOKENS, PANELS, HEAD_DIM)
        projected = jnp.transpose(projected, (1, 0, 2))
        query_rows = projected[:HEADS]
        key_rows = projected[kv_panel]
        value_rows = projected[kv_panel + KV_HEADS]
        bounds = jnp.cumsum(lengths[group_id])
        segment = jnp.sum((position[:, None] >= bounds[None, :]).astype(jnp.int32), axis=1)
        allowed = (segment[:, None] == segment[None, :]) & (position[None, :] <= position[:, None])
        scores = jnp.einsum('hqe,hke->hqk', query_rows, key_rows) * score_scale
        masked = jnp.where(allowed[None], scores, -jnp.inf)
        row_peak = jnp.max(masked, axis=2, keepdims=True)
        row_exp = jnp.exp(masked - row_peak)
        attn_probs = (row_exp / jnp.sum(row_exp, axis=2, keepdims=True)).astype(jnp.bfloat16)
        attn_probs = lax.optimization_barrier(attn_probs).astype(jnp.float32)
        context = jnp.einsum('hqk,hke->hqe', attn_probs, value_rows)
        outputs.append(jnp.transpose(context, (1, 0, 2)).reshape(TOKENS, HEADS * HEAD_DIM))
    return jnp.concatenate(outputs, axis=0)
```

```python
import functools

import jax
import jax.numpy as jnp
from jax import lax
from jax.experimental import pallas as pl
from jax.experimental.pallas import tpu as pltpu
from jax.sharding import PartitionSpec as P

F32 = jnp.float32
BF16 = jnp.bfloat16
VMEM = pl.BlockSpec(memory_space=pltpu.VMEM)
SMEM = pl.BlockSpec(memory_space=pltpu.SMEM)
ROOM = 48 * 1024 * 1024


def split(turn, pairs, tokens, *refs):
    outs, (blocks, sems) = refs[-2 - len(pairs) : -2], refs[-2:]
    group, core = lax.axis_index("grp"), lax.rem(lax.axis_index("tp"), 2)
    depth = outs[0].shape[1]
    copies = []
    for at, pair in enumerate(pairs):
        column = pl.ds(pl.multiple_of((group ^ jnp.where(core == 0, *pair)) * depth, depth), depth)
        copies.append(pltpu.make_async_copy(tokens.at[:, column], blocks.at[at], sems.at[at]))
        copies[-1].start()
    for at, out in enumerate(outs):
        copies[at].wait()
        for which in (0, 1):

            @pl.when(core == which)
            def _():
                block = blocks[at].astype(F32)
                firsts = range(turn * which, block.shape[0], 2 * turn)
                picked = jnp.concatenate([block[first : first + turn] for first in firsts], axis=0)
                out[...] = picked.astype(out.dtype)


def project(groups, *refs):
    token_refs, (own, sibling), outs = refs[:groups], refs[groups : groups + 2], refs[groups + 2 :]
    core = lax.rem(lax.axis_index("tp"), 2)
    slots, _, width = own.shape
    rows = token_refs[0].shape[0]
    stacked = jnp.concatenate([token_ref[...] for token_ref in token_refs], axis=0)
    for place, panels in ((core, own), (1 - core, sibling)):
        many = 1 if groups == 1 else 2
        for slot in range(0, slots, many):
            pair = jnp.concatenate([panels[slot + i] for i in range(many)], axis=1)
            part = jnp.dot(stacked, pair, preferred_element_type=F32)
            column = pl.ds(pl.multiple_of((place * slots + slot) * width, many * width), many * width)
            for at, out in enumerate(outs):
                out[:, column] = part[at * rows : (at + 1) * rows].astype(out.dtype)


def total(chips, steps, *refs):
    outs, turns = refs[-1 - chips : -1], refs[-1]
    value = refs[0][...]
    for ref in refs[1 : -1 - chips]:
        value += ref[...].astype(F32)
    turn, columns = value.shape[0] // chips, value.shape[1]
    for at in range(chips):
        turns[at, :turn] = value[at * turn : (at + 1) * turn]
    chip = lax.axis_index("tp") // 2
    for step, out in zip(steps, outs):
        seen = out.shape[0] // 2 // turn
        picked = jnp.concatenate([turns[jnp.maximum((chip ^ step) - back, 0)][:turn] for back in range(seen)], axis=0)
        picked = jnp.concatenate([picked[:, : columns // 2], picked[:, columns // 2 :]], axis=0)
        out[...] = picked.astype(out.dtype)


def lay_out(chips, steps, pieces, held):
    chip = lax.axis_index("tp") // 2
    held_rows, columns = held.shape[1:]
    piece_rows = pieces[0].shape[0] // 2
    for step, piece in zip(steps, pieces):
        value = piece[...].astype(F32)
        rest = jnp.zeros((held_rows - piece_rows, columns // 2), F32)
        for side in (0, 1):
            part = value[side * piece_rows : (side + 1) * piece_rows]
            part = jnp.concatenate([part, rest], axis=0).astype(held.dtype)
            held[chip ^ step, :, side * (columns // 2) : (side + 1) * (columns // 2)] = part


def visible(half, rows, pad, held_rows, piece_rows, lengths):
    member = lax.axis_index("tp")
    local = lax.broadcasted_iota(jnp.int32, (1, held_rows), 1)
    back = sum((local >= turns * rows).astype(jnp.int32) for turns in range(1, piece_rows // rows))
    key_at = (member // 2) * (2 * rows) + half * rows + local - back * (3 * rows)
    key_at = jnp.where(local < piece_rows, key_at, -1)
    query_at = lax.broadcasted_iota(jnp.int32, (pad, 1), 0) + member * rows
    bound = jnp.zeros((1, 1), jnp.int32)
    since = jnp.zeros((pad, 1), jnp.int32)
    for response in range(lengths.shape[1]):
        since = jnp.where(query_at >= bound, bound, since)
        bound = bound + lengths[:, response : response + 1]
    return (key_at <= query_at) & (key_at >= since)


def reader(panel_home, held, width):
    homes = panel_home[...]
    places = lax.broadcasted_iota(jnp.int32, homes.shape, 1)
    per_chip = held.shape[2] // width

    def panel(index):
        slot = jnp.sum(jnp.where(places == index, homes, 0))
        at = pl.multiple_of(lax.rem(slot, per_chip) * width, width)
        return held.at[slot // per_chip, :, pl.ds(at, width)]

    return panel


def score(queries, panel, heads, kv_count, pad, allowed):
    scores = []
    for head in range(heads):
        key = panel(heads + head // (heads // kv_count))[...]
        query = queries[head * pad : (head + 1) * pad]
        part = lax.dot_general(query, key, (((1,), (1,)), ((), ())), preferred_element_type=F32)
        scores.append(jnp.where(allowed, part * key.shape[1] ** -0.5, -1e30))
    return jnp.concatenate(scores, axis=0)


def mix(weights, panel, heads, kv_count, pad):
    parts = []
    for head in range(heads):
        value = panel(heads + kv_count + head // (heads // kv_count))[...]
        parts.append(jnp.dot(weights[head * pad : (head + 1) * pad], value, preferred_element_type=F32))
    return jnp.concatenate(parts, axis=0)


def attend_own(chips, steps, rows, heads, panel_home, lengths, *refs):
    pieces, (queries, peak, mass, mixed, held) = refs[:chips], refs[chips:]
    lay_out(chips, steps, pieces, held)
    width = queries.shape[1]
    kv_count = (panel_home.shape[1] - heads) // 2
    pad = queries.shape[0] // heads
    half = lax.rem(lax.axis_index("tp"), 2)
    allowed = visible(half, rows, pad, held.shape[1], pieces[0].shape[0] // 2, lengths)
    panel = reader(panel_home, held, width)
    query = jnp.concatenate([panel(head)[:pad] for head in range(heads)], axis=0)
    queries[...] = query
    scores = score(query, panel, heads, kv_count, pad, allowed)
    top = jnp.max(scores, axis=1, keepdims=True)
    weights = jnp.exp(scores - top)
    peak[...] = jnp.broadcast_to(top, peak.shape)
    mass[...] = jnp.broadcast_to(jnp.sum(weights, axis=1, keepdims=True), mass.shape)
    mixed[...] = mix(weights.astype(BF16), panel, heads, kv_count, pad)


def attend_rest(chips, steps, panel_home, lengths, queries, peak, mass, mixed, *refs):
    pieces, (out, held) = refs[:chips], refs[chips:]
    lay_out(chips, steps, pieces, held)
    rows, width = out.shape[0], queries.shape[1]
    heads = out.shape[1] // width
    kv_count = (panel_home.shape[1] - heads) // 2
    pad = queries.shape[0] // heads
    half = 1 - lax.rem(lax.axis_index("tp"), 2)
    allowed = visible(half, rows, pad, held.shape[1], pieces[0].shape[0] // 2, lengths)
    panel = reader(panel_home, held, width)
    scores = score(queries[...], panel, heads, kv_count, pad, allowed)
    before = peak[:, :1]
    top = jnp.maximum(before, jnp.max(scores, axis=1, keepdims=True))
    weights = jnp.exp(scores - top)
    kept = jnp.exp(before - top)
    whole = mass[:, :1] * kept + jnp.sum(weights, axis=1, keepdims=True)
    value = mixed[...] * kept + mix(weights.astype(BF16), panel, heads, kv_count, pad)
    value = value / whole
    for head in range(heads):
        out[:, head * width : (head + 1) * width] = value[head * pad : head * pad + rows]


def call(body, outs, in_specs, out_specs, scratch=(), flops=0, nbytes=0):
    return pl.pallas_call(
        body,
        out_shape=outs,
        in_specs=in_specs,
        out_specs=out_specs,
        scratch_shapes=scratch,
        compiler_params=pltpu.CompilerParams(vmem_limit_bytes=ROOM),
        cost_estimate=pl.CostEstimate(flops=flops, bytes_accessed=nbytes, transcendentals=0),
    )


def swap(x, axis, distance):
    size = lax.axis_size(axis)
    return lax.ppermute(x, axis, [(i, i ^ distance) for i in range(size)])


def swap_groups(x, pair):
    groups, members = lax.axis_size("grp"), lax.axis_size("tp")
    places = [(g * members + t, (g ^ pair[t % 2]) * members + t) for g in range(groups) for t in range(members)]
    return lax.ppermute(x, ("grp", "tp"), places)


def on_device(tokens, trainer_panels, panel_home, lengths):
    groups, members = lax.axis_size("grp"), lax.axis_size("tp")
    group, core = lax.axis_index("grp"), lax.rem(lax.axis_index("tp"), 2)
    chips = members // 2
    slots, depth, width = trainer_panels.shape
    rows, model = tokens.shape
    half, turn = rows // 2, rows // members
    columns = 2 * slots * width

    sibling = swap(trainer_panels, "tp", 1)
    pairs = [(0, 0), *zip(range(1, groups - 1), range(groups - 2, 0, -1)), (groups - 1, groups - 1)]
    if depth % 128 == 0:
        in_hbm = pltpu.with_memory_space_constraint(tokens, pltpu.HBM)

        def cut(pairs, *before):
            return list(
                call(
                    functools.partial(split, turn, pairs),
                    [jax.ShapeDtypeStruct((half, depth), BF16)] * len(pairs),
                    [pl.BlockSpec(memory_space=pltpu.HBM)] + [pl.BlockSpec(memory_space=pl.ANY)] * len(before),
                    [VMEM] * len(pairs),
                    scratch=[pltpu.VMEM((len(pairs), rows, depth), BF16), pltpu.SemaphoreType.DMA((len(pairs),))],
                    nbytes=2 * len(pairs) * rows * depth,
                )(in_hbm, *before)
            )

        far = cut(pairs[-1:])
        near = cut(pairs[1:-1], far[0])
        blocks = cut(pairs[:1], near[0]) + near + far
    else:
        turns = tokens.reshape(chips, 2, turn, model)
        blocks = [
            lax.dynamic_slice(
                turns, (0, core, 0, (group ^ jnp.where(core == 0, *pair)) * depth), (chips, 1, turn, depth)
            ).reshape(half, depth)
            for pair in pairs
        ]
    batches = [groups - 1], list(range(1, groups - 1))
    arrived = {step: swap_groups(blocks[step], pairs[step]) for steps in batches for step in steps}

    def products(token_blocks, dtype):
        return call(
            functools.partial(project, len(token_blocks)),
            [jax.ShapeDtypeStruct((half, columns), dtype)] * len(token_blocks),
            [VMEM] * (len(token_blocks) + 2),
            [VMEM] * len(token_blocks),
            flops=2 * len(token_blocks) * half * depth * columns,
            nbytes=2 * depth * columns,
        )(*token_blocks, trainer_panels, sibling)

    kept = products(blocks[:1], F32)
    parts = []
    for steps in batches:
        batch = [arrived[step] for step in steps]
        if not parts:
            kept, batch = lax.optimization_barrier((kept, batch))
        sent = products(batch, BF16)
        parts += [swap_groups(part, pairs[step]) for step, part in zip(steps, sent)]

    seen = min(chips, -(-(half - 1) // (2 * turn)) + 1)
    steps = list(range(chips // 2, chips)) + list(range(chips // 2 - 1, -1, -1))
    pieces = call(
        functools.partial(total, chips, steps),
        [jax.ShapeDtypeStruct((2 * seen * turn, columns // 2), BF16)] * chips,
        [VMEM] * groups,
        [VMEM] * chips,
        scratch=[pltpu.VMEM((chips, -(-turn // 8) * 8, columns), F32)],
        nbytes=2 * groups * half * columns,
    )(*kept, parts[0], *parts[:0:-1])
    pieces = [swap(piece, "tp", 2 * step) if step else piece for step, piece in zip(steps, pieces)]
    others = [swap(piece, "tp", 1) for piece in pieces[::-1]][::-1]
    held = pltpu.VMEM((chips, -(-seen * turn // 16) * 16, columns), BF16)
    homes = panel_home.reshape(1, -1)
    queries = members * -(-turn // 16) * 16
    so_far = call(
        functools.partial(attend_own, chips, steps, turn, members),
        [jax.ShapeDtypeStruct((queries, width), BF16)] + [jax.ShapeDtypeStruct((queries, width), F32)] * 3,
        [VMEM] * (2 + chips),
        [VMEM] * 4,
        scratch=[held],
        nbytes=2 * chips * half * columns,
    )(homes, lengths, *pieces)
    return call(
        functools.partial(attend_rest, chips, steps),
        jax.ShapeDtypeStruct((turn, members * width), F32),
        [VMEM] * (6 + chips),
        VMEM,
        scratch=[held],
        nbytes=2 * chips * half * columns,
    )(homes, lengths, *so_far, *others)


def solution(mesh):
    placed = (P("grp", None), P("tp", "grp", None), P(), P("grp", None))
    return jax.shard_map(
        on_device, mesh=mesh, in_specs=placed, out_specs=P(("grp", "tp"), None), check_vma=False
    )
```

```python
import functools

import jax
import jax.numpy as jnp
from jax import lax
from jax.experimental import pallas as pl
from jax.experimental.pallas import tpu as pltpu
from jax.sharding import PartitionSpec as P

F32 = jnp.float32
BF16 = jnp.bfloat16
VMEM = pl.BlockSpec(memory_space=pltpu.VMEM)
SMEM = pl.BlockSpec(memory_space=pltpu.SMEM)
ROOM = 48 * 1024 * 1024


def split(turn, pairs, tokens, *refs):
    outs, (blocks, sems) = refs[-2 - len(pairs) : -2], refs[-2:]
    group, core = lax.axis_index("grp"), lax.rem(lax.axis_index("tp"), 2)
    depth = outs[0].shape[1]
    copies = []
    for at, pair in enumerate(pairs):
        column = pl.ds(pl.multiple_of((group ^ jnp.where(core == 0, *pair)) * depth, depth), depth)
        copies.append(pltpu.make_async_copy(tokens.at[:, column], blocks.at[at], sems.at[at]))
        copies[-1].start()
    for at, out in enumerate(outs):
        copies[at].wait()
        for which in (0, 1):

            @pl.when(core == which)
            def _():
                block = blocks[at].astype(F32)
                firsts = range(turn * which, block.shape[0], 2 * turn)
                picked = jnp.concatenate([block[first : first + turn] for first in firsts], axis=0)
                out[...] = picked.astype(out.dtype)


def project(groups, *refs):
    token_refs, (own, sibling), outs = refs[:groups], refs[groups : groups + 2], refs[groups + 2 :]
    core = lax.rem(lax.axis_index("tp"), 2)
    slots, _, width = own.shape
    rows = token_refs[0].shape[0]
    stacked = jnp.concatenate([token_ref[...] for token_ref in token_refs], axis=0)
    for place, panels in ((core, own), (1 - core, sibling)):
        many = 1 if groups == 1 else 2
        for slot in range(0, slots, many):
            pair = jnp.concatenate([panels[slot + i] for i in range(many)], axis=1)
            part = jnp.dot(stacked, pair, preferred_element_type=F32)
            column = pl.ds(pl.multiple_of((place * slots + slot) * width, many * width), many * width)
            for at, out in enumerate(outs):
                out[:, column] = part[at * rows : (at + 1) * rows].astype(out.dtype)


def total(chips, steps, *refs):
    outs, turns = refs[-1 - chips : -1], refs[-1]
    value = refs[0][...]
    for ref in refs[1 : -1 - chips]:
        value += ref[...].astype(F32)
    turn, columns = value.shape[0] // chips, value.shape[1]
    for at in range(chips):
        turns[at, :turn] = value[at * turn : (at + 1) * turn]
    chip = lax.axis_index("tp") // 2
    for step, out in zip(steps, outs):
        seen = out.shape[0] // 2 // turn
        picked = jnp.concatenate([turns[jnp.maximum((chip ^ step) - back, 0)][:turn] for back in range(seen)], axis=0)
        picked = jnp.concatenate([picked[:, : columns // 2], picked[:, columns // 2 :]], axis=0)
        out[...] = picked.astype(out.dtype)


def lay_out(chips, steps, pieces, held):
    chip = lax.axis_index("tp") // 2
    held_rows, columns = held.shape[1:]
    piece_rows = pieces[0].shape[0] // 2
    for step, piece in zip(steps, pieces):
        value = piece[...].astype(F32)
        rest = jnp.zeros((held_rows - piece_rows, columns // 2), F32)
        for side in (0, 1):
            part = value[side * piece_rows : (side + 1) * piece_rows]
            part = jnp.concatenate([part, rest], axis=0).astype(held.dtype)
            held[chip ^ step, :, side * (columns // 2) : (side + 1) * (columns // 2)] = part


def visible(half, rows, pad, held_rows, piece_rows, lengths):
    member = lax.axis_index("tp")
    local = lax.broadcasted_iota(jnp.int32, (1, held_rows), 1)
    back = sum((local >= turns * rows).astype(jnp.int32) for turns in range(1, piece_rows // rows))
    key_at = (member // 2) * (2 * rows) + half * rows + local - back * (3 * rows)
    key_at = jnp.where(local < piece_rows, key_at, -1)
    query_at = lax.broadcasted_iota(jnp.int32, (pad, 1), 0) + member * rows
    bound = jnp.zeros((1, 1), jnp.int32)
    since = jnp.zeros((pad, 1), jnp.int32)
    for response in range(lengths.shape[1]):
        since = jnp.where(query_at >= bound, bound, since)
        bound = bound + lengths[:, response : response + 1]
    return (key_at <= query_at) & (key_at >= since)


def reader(panel_home, held, width):
    homes = panel_home[...]
    places = lax.broadcasted_iota(jnp.int32, homes.shape, 1)
    per_chip = held.shape[2] // width

    def panel(index):
        slot = jnp.sum(jnp.where(places == index, homes, 0))
        at = pl.multiple_of(lax.rem(slot, per_chip) * width, width)
        return held.at[slot // per_chip, :, pl.ds(at, width)]

    return panel


def score(queries, panel, heads, kv_count, pad, allowed):
    scores = []
    for head in range(heads):
        key = panel(heads + head // (heads // kv_count))[...]
        query = queries[head * pad : (head + 1) * pad]
        part = lax.dot_general(query, key, (((1,), (1,)), ((), ())), preferred_element_type=F32)
        scores.append(jnp.where(allowed, part * key.shape[1] ** -0.5, -1e30))
    return jnp.concatenate(scores, axis=0)


def mix(weights, panel, heads, kv_count, pad):
    parts = []
    for head in range(heads):
        value = panel(heads + kv_count + head // (heads // kv_count))[...]
        parts.append(jnp.dot(weights[head * pad : (head + 1) * pad], value, preferred_element_type=F32))
    return jnp.concatenate(parts, axis=0)


def attend_own(chips, steps, rows, heads, panel_home, lengths, *refs):
    pieces, (queries, peak, mass, mixed, held) = refs[:chips], refs[chips:]
    lay_out(chips, steps, pieces, held)
    width = queries.shape[1]
    kv_count = (panel_home.shape[1] - heads) // 2
    pad = queries.shape[0] // heads
    half = lax.rem(lax.axis_index("tp"), 2)
    allowed = visible(half, rows, pad, held.shape[1], pieces[0].shape[0] // 2, lengths)
    panel = reader(panel_home, held, width)
    query = jnp.concatenate([panel(head)[:pad] for head in range(heads)], axis=0)
    queries[...] = query
    scores = score(query, panel, heads, kv_count, pad, allowed)
    top = jnp.max(scores, axis=1, keepdims=True)
    weights = jnp.exp(scores - top)
    peak[...] = jnp.broadcast_to(top, peak.shape)
    mass[...] = jnp.broadcast_to(jnp.sum(weights, axis=1, keepdims=True), mass.shape)
    mixed[...] = mix(weights.astype(BF16), panel, heads, kv_count, pad)


def attend_rest(chips, steps, panel_home, lengths, queries, peak, mass, mixed, *refs):
    pieces, (out, held) = refs[:chips], refs[chips:]
    lay_out(chips, steps, pieces, held)
    rows, width = out.shape[0], queries.shape[1]
    heads = out.shape[1] // width
    kv_count = (panel_home.shape[1] - heads) // 2
    pad = queries.shape[0] // heads
    half = 1 - lax.rem(lax.axis_index("tp"), 2)
    allowed = visible(half, rows, pad, held.shape[1], pieces[0].shape[0] // 2, lengths)
    panel = reader(panel_home, held, width)
    scores = score(queries[...], panel, heads, kv_count, pad, allowed)
    before = peak[:, :1]
    top = jnp.maximum(before, jnp.max(scores, axis=1, keepdims=True))
    weights = jnp.exp(scores - top)
    kept = jnp.exp(before - top)
    whole = mass[:, :1] * kept + jnp.sum(weights, axis=1, keepdims=True)
    value = mixed[...] * kept + mix(weights.astype(BF16), panel, heads, kv_count, pad)
    value = value / whole
    for head in range(heads):
        out[:, head * width : (head + 1) * width] = value[head * pad : head * pad + rows]


def call(body, outs, in_specs, out_specs, scratch=(), flops=0, nbytes=0):
    return pl.pallas_call(
        body,
        out_shape=outs,
        in_specs=in_specs,
        out_specs=out_specs,
        scratch_shapes=scratch,
        compiler_params=pltpu.CompilerParams(vmem_limit_bytes=ROOM),
        cost_estimate=pl.CostEstimate(flops=flops, bytes_accessed=nbytes, transcendentals=0),
    )


def swap(x, axis, distance):
    size = lax.axis_size(axis)
    return lax.ppermute(x, axis, [(i, i ^ distance) for i in range(size)])


def swap_groups(x, pair):
    groups, members = lax.axis_size("grp"), lax.axis_size("tp")
    places = [(g * members + t, (g ^ pair[t % 2]) * members + t) for g in range(groups) for t in range(members)]
    return lax.ppermute(x, ("grp", "tp"), places)


def on_device(tokens, trainer_panels, panel_home, lengths):
    groups, members = lax.axis_size("grp"), lax.axis_size("tp")
    group, core = lax.axis_index("grp"), lax.rem(lax.axis_index("tp"), 2)
    chips = members // 2
    slots, depth, width = trainer_panels.shape
    rows, model = tokens.shape
    half, turn = rows // 2, rows // members
    columns = 2 * slots * width

    sibling = swap(trainer_panels, "tp", 1)
    pairs = [(0, 0), *zip(range(groups - 2, 0, -1), range(1, groups - 1)), (groups - 1, groups - 1)]
    if depth % 128 == 0:
        in_hbm = pltpu.with_memory_space_constraint(tokens, pltpu.HBM)

        def cut(pairs, *before):
            return list(
                call(
                    functools.partial(split, turn, pairs),
                    [jax.ShapeDtypeStruct((half, depth), BF16)] * len(pairs),
                    [pl.BlockSpec(memory_space=pltpu.HBM)] + [pl.BlockSpec(memory_space=pl.ANY)] * len(before),
                    [VMEM] * len(pairs),
                    scratch=[pltpu.VMEM((len(pairs), rows, depth), BF16), pltpu.SemaphoreType.DMA((len(pairs),))],
                    nbytes=2 * len(pairs) * rows * depth,
                )(in_hbm, *before)
            )

        far = cut(pairs[-1:])
        near = cut(pairs[1:-1], far[0])
        blocks = cut(pairs[:1], near[0]) + near + far
    else:
        turns = tokens.reshape(chips, 2, turn, model)
        blocks = [
            lax.dynamic_slice(
                turns, (0, core, 0, (group ^ jnp.where(core == 0, *pair)) * depth), (chips, 1, turn, depth)
            ).reshape(half, depth)
            for pair in pairs
        ]
    batches = [groups - 1], list(range(1, groups - 1))
    arrived = {step: swap_groups(blocks[step], pairs[step]) for steps in batches for step in steps}

    def products(token_blocks, dtype):
        return call(
            functools.partial(project, len(token_blocks)),
            [jax.ShapeDtypeStruct((half, columns), dtype)] * len(token_blocks),
            [VMEM] * (len(token_blocks) + 2),
            [VMEM] * len(token_blocks),
            flops=2 * len(token_blocks) * half * depth * columns,
            nbytes=2 * depth * columns,
        )(*token_blocks, trainer_panels, sibling)

    kept = products(blocks[:1], F32)
    parts = []
    for steps in batches:
        batch = [arrived[step] for step in steps]
        if not parts:
            kept, batch = lax.optimization_barrier((kept, batch))
        sent = products(batch, BF16)
        parts += [swap_groups(part, pairs[step]) for step, part in zip(steps, sent)]

    seen = min(chips, -(-(half - 1) // (2 * turn)) + 1)
    steps = list(range(chips // 2, chips)) + list(range(chips // 2 - 1, -1, -1))
    pieces = call(
        functools.partial(total, chips, steps),
        [jax.ShapeDtypeStruct((2 * seen * turn, columns // 2), BF16)] * chips,
        [VMEM] * groups,
        [VMEM] * chips,
        scratch=[pltpu.VMEM((chips, -(-turn // 8) * 8, columns), F32)],
        nbytes=2 * groups * half * columns,
    )(*kept, parts[0], *parts[:0:-1])
    pieces = [swap(piece, "tp", 2 * step) if step else piece for step, piece in zip(steps, pieces)]
    others = [swap(piece, "tp", 1) for piece in pieces[::-1]][::-1]
    held = pltpu.VMEM((chips, -(-seen * turn // 16) * 16, columns), BF16)
    homes = panel_home.reshape(1, -1)
    queries = members * -(-turn // 16) * 16
    so_far = call(
        functools.partial(attend_own, chips, steps, turn, members),
        [jax.ShapeDtypeStruct((queries, width), BF16)] + [jax.ShapeDtypeStruct((queries, width), F32)] * 3,
        [VMEM] * (2 + chips),
        [VMEM] * 4,
        scratch=[held],
        nbytes=2 * chips * half * columns,
    )(homes, lengths, *pieces)
    return call(
        functools.partial(attend_rest, chips, steps),
        jax.ShapeDtypeStruct((turn, members * width), F32),
        [VMEM] * (6 + chips),
        VMEM,
        scratch=[held],
        nbytes=2 * chips * half * columns,
    )(homes, lengths, *so_far, *others)


def solution(mesh):
    placed = (P("grp", None), P("tp", "grp", None), P(), P("grp", None))
    return jax.shard_map(
        on_device, mesh=mesh, in_specs=placed, out_specs=P(("grp", "tp"), None), check_vma=False
    )
```
